32 devices in a mesh: row: 4 (over z), col: 8 (over y, x, core).
Axes of the slice: x: 2, y: 2, z: 4, core: 2. Of those that a mesh axis runs over, the one named last changes fastest.
Arguments:
- coefficients: float32 [3, 7, 1024, 3072], P(None, None, 'col', 'row'), may hold values from -0.6 to 0.6
- basis_values: float32 [4, 4], replicated, may hold values from 0.05 to 1
- basis_slopes: float32 [4, 4], replicated, may hold values from -150 to 150
- band_offsets: int32 [4], replicated, may hold values from 0 to 3, as said below
Outputs:
- nonlinear_terms: float32 [3, 4, 1024, 3072], P(None, None, 'col', 'row')
The draws below stay inside these ranges and needn't reach their ends.
Inputs may be any that keep to these rules, and one draw needn't show every extreme that they name: `band_offsets`: nondecreasing over the planes; the first is 0 and the last 3.
All inputs are finite; a program needn't handle non-finite values.
Results may differ from the reference program's by a relative error of at most 0.0095.
Values may be sent and summed in bfloat16 or wider, within the bound.
A program may use at most 128 MiB of HBM per device.

```python
import math
import jax
import jax.numpy as jnp
from jax import lax

NZ = 1536
BAND = 4
MX = 1024
PX = 3072
PZ = 2304
PY = 4
SPL = 7


def draw_coefficients(key, part):
    stream_wave = jnp.arange(MX, dtype=jnp.int32).astype(jnp.float32) * 0.25
    mode_index = jnp.arange(2 * NZ, dtype=jnp.int32) // 2
    span_wave = jnp.where(mode_index < NZ // 2, mode_index, mode_index - NZ).astype(jnp.float32) * (2.0 / 3.0)
    radius = jnp.sqrt(stream_wave[:, None] * stream_wave[:, None] + span_wave[None, :] * span_wave[None, :])
    envelope = 0.15 / (1.0 + radius)
    shape = (3, SPL, MX, 2 * NZ)
    base = jnp.clip(jax.random.normal(key, shape, jnp.float32), -4.0, 4.0)
    return base * envelope


def draw_band_offsets(key, part):
    inner = jnp.sort(jax.random.randint(key, (PY,), 0, PY, dtype=jnp.int32))
    position = jnp.arange(PY, dtype=jnp.int32)
    return jnp.where(position == 0, 0, jnp.where(position == PY - 1, PY - 1, inner)).astype(jnp.int32)


def setup_inputs(seed: int = 0) -> dict:
    streams_of = jax.random.split(jax.random.key(seed), 5)
    coefficients = draw_coefficients(jax.random.fold_in(streams_of[4], 71), 0)
    basis_values = jnp.clip(jax.random.uniform(streams_of[1], (PY, BAND), jnp.float32, 0.05, 1.0), 0.05, 1.0)
    basis_slopes = jnp.clip(jax.random.uniform(streams_of[2], (PY, BAND), jnp.float32, -150.0, 150.0), -150.0, 150.0)
    band_offsets = draw_band_offsets(jax.random.fold_in(streams_of[4], 71), 0)
    return {"coefficients": coefficients, "basis_values": basis_values, "basis_slopes": basis_slopes, "band_offsets": band_offsets}


stream_unit = 0.25
span_unit = 2.0 / 3.0


def collocation(offsets, weights, spline_total):
    band_width = weights.shape[1]
    selected = jnp.arange(spline_total, dtype=jnp.int32)[None, None, :] == (offsets[:, None, None] + jnp.arange(band_width, dtype=jnp.int32)[None, :, None])
    return jnp.sum(jnp.where(selected, weights[:, :, None], 0.0), axis=1)


def signed_wave(mode_index, mode_total):
    signed = jnp.where(mode_index < mode_total // 2, mode_index, mode_index - mode_total)
    return signed.astype(jnp.float32) * span_unit


def vorticity(velocity, slopes, stream_wave, span_wave):
    real_part = velocity[:, 0].astype(jnp.float32)
    imag_part = velocity[:, 1].astype(jnp.float32)
    slope_real = slopes[:, 0].astype(jnp.float32)
    slope_imag = slopes[:, 1].astype(jnp.float32)
    reals = [-span_wave * imag_part[1] - slope_real[1],
             -(stream_wave * imag_part[2] - span_wave * imag_part[0]),
             slope_real[0] + stream_wave * imag_part[1]]
    imags = [span_wave * real_part[1] - slope_imag[1],
             stream_wave * real_part[2] - span_wave * real_part[0],
             slope_imag[0] - stream_wave * real_part[1]]
    return jnp.stack([jnp.stack([reals[k], imags[k]]) for k in range(3)]).astype(jnp.bfloat16)


def span_tables(mode_total, points):
    mode_index = jnp.arange(mode_total, dtype=jnp.int32)
    signed = jnp.where(mode_index < mode_total // 2, mode_index, mode_index - mode_total)
    point_index = jnp.arange(points, dtype=jnp.int32)
    angles = jnp.mod(signed[:, None] * point_index[None, :], points).astype(jnp.float32) * (2.0 * math.pi / points)
    cosines = jnp.cos(angles)
    sine_wave = jnp.sin(angles)
    return cosines.astype(jnp.bfloat16), (sine_wave - cosines).astype(jnp.bfloat16), (cosines + sine_wave).astype(jnp.bfloat16)


def stream_tables(mode_total, points):
    mode_index = jnp.arange(mode_total, dtype=jnp.int32)
    point_index = jnp.arange(points, dtype=jnp.int32)
    angles = jnp.mod(mode_index[:, None] * point_index[None, :], points).astype(jnp.float32) * (2.0 * math.pi / points)
    forward_table = jnp.stack([jnp.cos(angles), -jnp.sin(angles)]).astype(jnp.bfloat16)
    weight = jnp.where(mode_index == 0, 1.0, 2.0).astype(jnp.float32)
    inverse_table = (forward_table.astype(jnp.float32) * weight[None, :, None]).astype(jnp.bfloat16)
    return forward_table, inverse_table


def contract(left, table, form):
    return jnp.einsum(form, left.astype(jnp.float32), table.astype(jnp.float32), precision=lax.Precision.HIGHEST)


def inverse_span(fields, cosine_table, minus_table, plus_table):
    real_part = fields[:, 0]
    imag_part = fields[:, 1]
    summed = (real_part.astype(jnp.float32) + imag_part.astype(jnp.float32)).astype(jnp.bfloat16)
    common = contract(summed, cosine_table, "...q,qz->...z")
    real_out = common - contract(imag_part, plus_table, "...q,qz->...z")
    imag_out = common + contract(real_part, minus_table, "...q,qz->...z")
    return jnp.stack([real_out, imag_out], axis=1).astype(jnp.bfloat16)


def forward_span(spectral_x, cosine_table, minus_table, plus_table):
    real_part = spectral_x[:, 0]
    imag_part = spectral_x[:, 1]
    summed = (real_part.astype(jnp.float32) + imag_part.astype(jnp.float32)).astype(jnp.bfloat16)
    common = contract(summed, cosine_table, "...z,qz->...q")
    real_out = common + contract(imag_part, minus_table, "...z,qz->...q")
    imag_out = common - contract(real_part, plus_table, "...z,qz->...q")
    return jnp.stack([real_out, imag_out], axis=1)


def cross_product(physical):
    flow_part = physical[:3]
    twist_part = physical[3:]
    return jnp.stack([flow_part[1] * twist_part[2] - flow_part[2] * twist_part[1],
                      flow_part[2] * twist_part[0] - flow_part[0] * twist_part[2],
                      flow_part[0] * twist_part[1] - flow_part[1] * twist_part[0]]).astype(jnp.bfloat16)


def reference(coefficients, basis_values, basis_slopes, band_offsets):
    split_coefficients = jnp.moveaxis(coefficients.reshape(3, SPL, MX, NZ, 2), 4, 1)
    value_map = collocation(band_offsets, basis_values, SPL)
    slope_map = collocation(band_offsets, basis_slopes, SPL)
    velocity = jnp.einsum("js,cpsxz->cpjxz", value_map, split_coefficients, precision=lax.Precision.HIGHEST).astype(jnp.bfloat16)
    slopes = jnp.einsum("js,cpsxz->cpjxz", slope_map, split_coefficients[0::2], precision=lax.Precision.HIGHEST).astype(jnp.bfloat16)
    stream_wave = (jnp.arange(MX, dtype=jnp.int32).astype(jnp.float32) * stream_unit)[:, None]
    span_wave = signed_wave(jnp.arange(NZ, dtype=jnp.int32), NZ)
    cosine_table, minus_table, plus_table = span_tables(NZ, PZ)
    forward_table, inverse_table = stream_tables(MX, PX)
    norm_factor = 1.0 / (PX * PZ)

    def plane_terms(plane_data):
        plane_velocity, plane_slopes = plane_data
        vortex = vorticity(plane_velocity, plane_slopes, stream_wave, span_wave)
        fields = jnp.concatenate([plane_velocity, vortex], axis=0)
        span_grid = inverse_span(fields, cosine_table, minus_table, plus_table)
        physical = contract(span_grid, inverse_table, "fpmz,pmw->fzw")
        products = cross_product(physical)
        spectral_x = contract(products, forward_table, "czw,pmw->cpmz").astype(jnp.bfloat16)
        return forward_span(spectral_x, cosine_table, minus_table, plus_table) * norm_factor

    result = lax.map(plane_terms, (jnp.moveaxis(velocity, 2, 0), jnp.moveaxis(slopes, 2, 0)))
    result = jnp.moveaxis(result, 0, 2)
    return jnp.moveaxis(result, 1, 4).reshape(3, PY, MX, 2 * NZ)
```

```python
import functools
import math

import jax
import jax.numpy as jnp
import ml_dtypes
import numpy as np
from jax import lax
from jax.experimental import pallas as pl
from jax.experimental.pallas import tpu as pltpu
from jax.sharding import PartitionSpec as P

stream_unit = 0.25
span_unit = 2.0 / 3.0
VMEM_LIMIT = 56 * 1024 * 1024
BF = jnp.bfloat16
F32 = jnp.float32


def span_tables(mode_total, points):
    mode = np.arange(mode_total)
    signed = np.where(mode < mode_total // 2, mode, mode - mode_total)
    odd = 2 * np.arange(points // 2) + 1
    angle = np.mod(odd[:, None] * signed[None, :], 2 * points) * (math.pi / points)
    return np.cos(angle).astype(ml_dtypes.bfloat16), np.sin(angle).astype(ml_dtypes.bfloat16)


def stream_tables(mode_total, points):
    mode = np.arange(mode_total)
    odd = 2 * np.arange(points // 2) + 1
    angle = np.mod(mode[:, None] * odd[None, :], 2 * points) * (math.pi / points)
    return np.cos(angle).astype(ml_dtypes.bfloat16), (-np.sin(angle)).astype(ml_dtypes.bfloat16)


def split_table(count):
    table = np.zeros((2, count, 2 * count), ml_dtypes.bfloat16)
    index = np.arange(count)
    table[0, index, 2 * index] = 1
    table[1, index, 2 * index + 1] = 1
    return table.reshape(2 * count, 2 * count)


def dot(left, right):
    return jnp.dot(left, right, preferred_element_type=F32)


def collocate_kernel(values, slopes, offsets, coef, first, second):
    planes = values.shape[0]
    for j in range(planes):
        base = offsets[j]

        def total(weights, c):
            return sum(
                weights[j, t] * coef[c, base + t] for t in range(weights.shape[1])
            ).astype(BF)

        first[j, 0] = total(values, 0)
        first[j, 1] = total(values, 2)
        second[j, 0] = total(values, 1)
        second[j, 1] = total(slopes, 0)
        second[j, 2] = total(slopes, 2)


def collocate(coefficients, values, slopes, offsets, rows):
    _, splines, stream_local, width = coefficients.shape
    planes = values.shape[0]
    smem = pl.BlockSpec(memory_space=pltpu.SMEM)
    return pl.pallas_call(
        collocate_kernel,
        grid=(stream_local // rows,),
        in_specs=[smem, smem, smem, pl.BlockSpec((3, splines, rows, width), lambda i: (0, 0, i, 0))],
        out_specs=[
            pl.BlockSpec((planes, 2, rows, width), lambda i: (0, 0, i, 0)),
            pl.BlockSpec((planes, 3, rows, width), lambda i: (0, 0, i, 0)),
        ],
        out_shape=[
            jax.ShapeDtypeStruct((planes, 2, stream_local, width), BF),
            jax.ShapeDtypeStruct((planes, 3, stream_local, width), BF),
        ],
        compiler_params=pltpu.CompilerParams(vmem_limit_bytes=VMEM_LIMIT),
        name="collocate",
    )(values, slopes, offsets, coefficients)


def inverse_kernel(group, span_modes, x, stream_wave, split, cosine, sine, out, modes):
    rows, sent, stream_local, width = x.shape
    half = width // 2

    @pl.when(pl.program_id(0) == 0)
    def _():
        wave_x = stream_wave[...]

        def body(r, carry):
            flat = x[r].reshape(sent * stream_local, width)
            parts = lax.dot_general(
                split[...], flat, (((1,), (1,)), ((), ())), preferred_element_type=F32
            )
            field = lambda k: (
                parts[:half, k * stream_local : (k + 1) * stream_local],
                parts[half:, k * stream_local : (k + 1) * stream_local],
            )
            mode = r * half + lax.broadcasted_iota(jnp.int32, (half, stream_local), 0)
            signed = jnp.where(mode < span_modes // 2, mode, mode - span_modes)
            wave_z = signed.astype(F32) * span_unit
            if group == 0:
                (ur, ui), (wr, wi) = field(0), field(1)
                fields = [
                    (ur, ui),
                    (wr, wi),
                    (-(wave_x * wi - wave_z * ui), wave_x * wr - wave_z * ur),
                ]
            else:
                (vr, vi), (sur, sui), (swr, swi) = field(0), field(1), field(2)
                fields = [
                    (vr, vi),
                    (-wave_z * vi - swr, wave_z * vr - swi),
                    (sur + wave_x * vi, sui - wave_x * vr),
                ]
            here = pl.ds(pl.multiple_of(r * half, 16), half)
            for f in range(3):
                for p in range(2):
                    at = (p * 3 + f) * stream_local
                    modes[here, at : at + stream_local] = fields[f][p].astype(BF)
            return carry

        lax.fori_loop(0, rows, body, 0)

    by_cosine = dot(cosine[...], modes[...])
    by_sine = dot(sine[...], modes[...])
    part = 3 * stream_local
    pairs = [
        (by_cosine[:, :part], -by_sine[:, part:]),
        (by_cosine[:, part:], by_sine[:, :part]),
    ]
    block = out.shape[3] // 2
    for p, (even, odd) in enumerate(pairs):
        plus = (even + odd).astype(BF)
        minus = (even - odd).astype(BF)
        for d in range(out.shape[0]):
            for f in range(3):
                lanes = slice(f * stream_local, (f + 1) * stream_local)
                out[d, f, p, :block] = plus[d * block : (d + 1) * block, lanes]
                out[d, f, p, block:] = minus[d * block : (d + 1) * block, lanes]


def inverse_span(group, x, stream_wave, split, cosine, sine, col_count):
    rows, sent, stream_local, width = x.shape
    half_points, span_modes = cosine.shape
    block = half_points // col_count
    step = 2
    whole = lambda a: pl.BlockSpec(a.shape, lambda i: (0,) * a.ndim)
    table = pl.BlockSpec((step * block, span_modes), lambda i: (i, 0))
    return pl.pallas_call(
        functools.partial(inverse_kernel, group, span_modes),
        grid=(col_count // step,),
        in_specs=[whole(x), whole(stream_wave), whole(split), table, table],
        out_specs=pl.BlockSpec(
            (step, 3, 2, 2 * block, stream_local), lambda i: (i, 0, 0, 0, 0)
        ),
        out_shape=jax.ShapeDtypeStruct((col_count, 3, 2, 2 * block, stream_local), BF),
        scratch_shapes=[pltpu.VMEM((span_modes, 6 * stream_local), BF)],
        compiler_params=pltpu.CompilerParams(vmem_limit_bytes=VMEM_LIMIT),
        cost_estimate=pl.CostEstimate(
            flops=2 * 12 * stream_local * span_modes * half_points,
            bytes_accessed=4 * half_points * span_modes + 4 * x.size,
            transcendentals=0,
        ),
        name="inverse_span",
    )(x, stream_wave, split, cosine, sine)


def product_kernel(chunk, ga, gb, wave_c, wave_s, back_c, back_s, o0, o1, o2, reals, imags, acc_re, acc_im):
    cols, _, _, _, hb, lanes = ga.shape
    per = 2 * hb
    for g, ref in enumerate((ga, gb)):
        for f in range(3):
            row = (g * 3 + f) * per
            for d in range(cols):
                at = slice(d * lanes, (d + 1) * lanes)
                for s in range(2):
                    reals[row + s * hb : row + (s + 1) * hb, at] = ref[d, f, 0, s]
                    imags[row + s * hb : row + (s + 1) * hb, at] = ref[d, f, 1, s]
    points = wave_c.shape[1]
    for b in range(points // chunk):
        xs = slice(b * chunk, (b + 1) * chunk)
        even = dot(reals[...], wave_c[:, xs])
        odd = dot(imags[...], wave_s[:, xs])
        products = []
        for phys in (even + odd, even - odd):
            u, w, wy, v, wx, wz = [phys[k * per : (k + 1) * per] for k in range(6)]
            products.append((v * wz - w * wy, w * wx - u * wz, u * wy - v * wx))
        sums = []
        diffs = []
        for c in range(3):
            total = products[0][c] + products[1][c]
            gap = products[0][c] - products[1][c]
            sums += [total[:hb] + total[hb:], total[:hb] - total[hb:]]
            diffs += [gap[:hb] + gap[hb:], gap[:hb] - gap[hb:]]
        re = dot(jnp.concatenate(sums, axis=0).astype(BF), back_c[xs, :])
        im = dot(jnp.concatenate(diffs, axis=0).astype(BF), back_s[xs, :])
        if b == 0:
            acc_re[...] = re
            acc_im[...] = im
        else:
            acc_re[...] += re
            acc_im[...] += im
    for c, out in enumerate((o0, o1, o2)):
        for s in range(2):
            row = (c * 2 + s) * hb
            for d in range(cols):
                at = slice(d * lanes, (d + 1) * lanes)
                out[d, 0, s] = acc_re[row : row + hb, at].astype(BF)
                out[d, 1, s] = acc_im[row : row + hb, at].astype(BF)


def products(ga, gb, tables, hb, chunk):
    cols, _, _, points, lanes = ga.shape
    half = points // 2
    shape = (cols, 3, 2, 2, half, lanes)
    ga, gb = ga.reshape(shape), gb.reshape(shape)
    modes = cols * lanes
    spec = pl.BlockSpec((cols, 3, 2, 2, hb, lanes), lambda i: (0, 0, 0, 0, i, 0))
    out_spec = pl.BlockSpec((cols, 2, 2, hb, lanes), lambda i: (0, 0, 0, i, 0))
    whole = lambda a: pl.BlockSpec(a.shape, lambda i: (0, 0), pipeline_mode=pl.Buffered(1))
    stream_half = tables[0].shape[1]
    return pl.pallas_call(
        functools.partial(product_kernel, chunk),
        grid=(half // hb,),
        in_specs=[spec, spec] + [whole(t) for t in tables],
        out_specs=[out_spec] * 3,
        out_shape=[jax.ShapeDtypeStruct((cols, 2, 2, half, lanes), BF)] * 3,
        scratch_shapes=[
            pltpu.VMEM((12 * hb, modes), BF),
            pltpu.VMEM((12 * hb, modes), BF),
            pltpu.VMEM((6 * hb, modes), F32),
            pltpu.VMEM((6 * hb, modes), F32),
        ],
        compiler_params=pltpu.CompilerParams(vmem_limit_bytes=VMEM_LIMIT),
        cost_estimate=pl.CostEstimate(
            flops=2 * 36 * half * modes * stream_half,
            bytes_accessed=8 * modes * stream_half + 36 * 2 * points * modes,
            transcendentals=0,
        ),
        name="products",
    )(ga, gb, *tables)


def forward_kernel(norm, spectral, split, cosine, sine, out, plus, minus):
    cols, _, _, block, lanes = spectral.shape

    @pl.when(pl.program_id(0) == 0)
    def _():
        for d in range(cols):
            here = slice(d * block, (d + 1) * block)
            for p in range(2):
                at = slice(p * lanes, (p + 1) * lanes)
                plus[here, at] = spectral[d, p, 0]
                minus[here, at] = spectral[d, p, 1]

    by_cosine = dot(cosine[...], plus[...])
    by_sine = dot(sine[...], minus[...])
    re = (by_cosine[:, :lanes] + by_sine[:, lanes:]) * norm
    im = (by_cosine[:, lanes:] - by_sine[:, :lanes]) * norm
    parts = jnp.concatenate([re, im], axis=0).astype(BF)
    out[0] = lax.dot_general(
        parts, split[...], (((0,), (0,)), ((), ())), preferred_element_type=F32
    ).astype(BF)


def forward_span(spectral, split, cosine, sine, norm, row_count):
    cols, _, _, block, lanes = spectral.shape
    span_modes, half_points = cosine.shape
    width = 2 * span_modes // row_count
    whole = lambda a: pl.BlockSpec(a.shape, lambda i: (0,) * a.ndim)
    table = pl.BlockSpec((width // 2, half_points), lambda i: (i, 0))
    return pl.pallas_call(
        functools.partial(forward_kernel, norm),
        grid=(row_count,),
        in_specs=[whole(spectral), whole(split), table, table],
        out_specs=pl.BlockSpec((1, lanes, width), lambda i: (i, 0, 0)),
        out_shape=jax.ShapeDtypeStruct((row_count, lanes, width), BF),
        scratch_shapes=[pltpu.VMEM((half_points, 2 * lanes), BF)] * 2,
        compiler_params=pltpu.CompilerParams(vmem_limit_bytes=VMEM_LIMIT),
        cost_estimate=pl.CostEstimate(
            flops=2 * 4 * lanes * span_modes * half_points,
            bytes_accessed=4 * half_points * span_modes + 4 * spectral.size,
            transcendentals=0,
        ),
        name="forward_span",
    )(spectral, split, cosine, sine)


def exchange(x, axis):
    return lax.all_to_all(x, axis, split_axis=0, concat_axis=0, tiled=True)


def on_device(coefficients, basis_values, basis_slopes, band_offsets):
    row_count = lax.axis_size("row")
    col_count = lax.axis_size("col")
    stream_local = coefficients.shape[2]
    span_local = coefficients.shape[3] // 2
    stream_modes = stream_local * col_count
    span_modes = span_local * row_count
    span_points = 3 * span_modes // 2
    stream_points = 3 * stream_modes
    cosine, sine = span_tables(span_modes, span_points)
    wave_c, wave_s = stream_tables(stream_modes, stream_points)
    weight = np.where(np.arange(stream_modes) == 0, 1.0, 2.0)[:, None].astype(ml_dtypes.bfloat16)
    stream = [wave_c * weight, wave_s * weight, wave_c.T, wave_s.T]
    stream = [jnp.asarray(np.ascontiguousarray(t)) for t in stream]
    split = jnp.asarray(split_table(span_local))
    span = jnp.asarray(cosine), jnp.asarray(sine)
    back = jnp.asarray(np.ascontiguousarray(cosine.T)), jnp.asarray(np.ascontiguousarray(sine.T))
    norm = 1.0 / (stream_points * span_points)

    stream_index = lax.axis_index("col") * stream_local + jnp.arange(stream_local, dtype=jnp.int32)
    stream_wave = (stream_index.astype(F32) * stream_unit)[None, :]

    sent = collocate(coefficients, basis_values, basis_slopes, band_offsets, 32)
    grids = []
    for group in range(2):
        modes = exchange(sent[group], "row")
        grid = inverse_span(group, modes, stream_wave, split, *span, col_count)
        grids.append(exchange(grid, "col"))
    half = span_points // 2 // col_count
    terms = products(*grids, stream, 48 if half % 48 == 0 else half, 512)
    results = []
    for term in terms:
        spectrum = forward_span(exchange(term, "col"), split, *back, norm, row_count)
        results.append(exchange(spectrum, "row"))
    return jnp.stack(results).astype(F32)


def solution(mesh):
    placed = (P(None, None, "col", "row"), P(), P(), P())
    return jax.shard_map(
        on_device,
        mesh=mesh,
        in_specs=placed,
        out_specs=P(None, None, "col", "row"),
        check_vma=False,
    )
```

```python
import functools
import math

import jax
import jax.numpy as jnp
import ml_dtypes
import numpy as np
from jax import lax
from jax.experimental import pallas as pl
from jax.experimental.pallas import tpu as pltpu
from jax.sharding import PartitionSpec as P

stream_unit = 0.25
span_unit = 2.0 / 3.0
VMEM_LIMIT = 56 * 1024 * 1024
BF = jnp.bfloat16
F32 = jnp.float32


def span_tables(mode_total, points):
    mode = np.arange(mode_total)
    signed = np.where(mode < mode_total // 2, mode, mode - mode_total)
    odd = 2 * np.arange(points // 2) + 1
    angle = np.mod(odd[:, None] * signed[None, :], 2 * points) * (math.pi / points)
    return np.cos(angle).astype(ml_dtypes.bfloat16), np.sin(angle).astype(ml_dtypes.bfloat16)


def stream_tables(mode_total, points):
    mode = np.arange(mode_total)
    odd = 2 * np.arange(points // 2) + 1
    angle = np.mod(mode[:, None] * odd[None, :], 2 * points) * (math.pi / points)
    return np.cos(angle).astype(ml_dtypes.bfloat16), (-np.sin(angle)).astype(ml_dtypes.bfloat16)


def split_table(count):
    table = np.zeros((2, count, 2 * count), ml_dtypes.bfloat16)
    index = np.arange(count)
    table[0, index, 2 * index] = 1
    table[1, index, 2 * index + 1] = 1
    return table.reshape(2 * count, 2 * count)


def dot(left, right):
    return jnp.dot(left, right, preferred_element_type=F32)


def collocate_kernel(values, slopes, offsets, coef, first, second):
    planes = values.shape[0]
    for j in range(planes):
        base = offsets[j]

        def total(weights, c):
            return sum(
                weights[j, t] * coef[c, base + t] for t in range(weights.shape[1])
            ).astype(BF)

        first[j, 0] = total(values, 0)
        first[j, 1] = total(values, 2)
        second[j, 0] = total(values, 1)
        second[j, 1] = total(slopes, 0)
        second[j, 2] = total(slopes, 2)


def collocate(coefficients, values, slopes, offsets, rows):
    _, splines, stream_local, width = coefficients.shape
    planes = values.shape[0]
    smem = pl.BlockSpec(memory_space=pltpu.SMEM)
    return pl.pallas_call(
        collocate_kernel,
        grid=(stream_local // rows,),
        in_specs=[smem, smem, smem, pl.BlockSpec((3, splines, rows, width), lambda i: (0, 0, i, 0))],
        out_specs=[
            pl.BlockSpec((planes, 2, rows, width), lambda i: (0, 0, i, 0)),
            pl.BlockSpec((planes, 3, rows, width), lambda i: (0, 0, i, 0)),
        ],
        out_shape=[
            jax.ShapeDtypeStruct((planes, 2, stream_local, width), BF),
            jax.ShapeDtypeStruct((planes, 3, stream_local, width), BF),
        ],
        compiler_params=pltpu.CompilerParams(vmem_limit_bytes=VMEM_LIMIT),
        name="collocate",
    )(values, slopes, offsets, coefficients)


def inverse_kernel(group, span_modes, x, stream_wave, split, cosine, sine, out, modes):
    rows, sent, stream_local, width = x.shape
    half = width // 2

    @pl.when(pl.program_id(0) == 0)
    def _():
        wave_x = stream_wave[...]

        def body(r, carry):
            flat = x[r].reshape(sent * stream_local, width)
            parts = lax.dot_general(
                split[...], flat, (((1,), (1,)), ((), ())), preferred_element_type=F32
            )
            field = lambda k: (
                parts[:half, k * stream_local : (k + 1) * stream_local],
                parts[half:, k * stream_local : (k + 1) * stream_local],
            )
            mode = r * half + lax.broadcasted_iota(jnp.int32, (half, stream_local), 0)
            signed = jnp.where(mode < span_modes // 2, mode, mode - span_modes)
            wave_z = signed.astype(F32) * span_unit
            if group == 0:
                (ur, ui), (wr, wi) = field(0), field(1)
                fields = [
                    (ur, ui),
                    (wr, wi),
                    (-(wave_x * wi - wave_z * ui), wave_x * wr - wave_z * ur),
                ]
            else:
                (vr, vi), (sur, sui), (swr, swi) = field(0), field(1), field(2)
                fields = [
                    (vr, vi),
                    (-wave_z * vi - swr, wave_z * vr - swi),
                    (sur + wave_x * vi, sui - wave_x * vr),
                ]
            here = pl.ds(pl.multiple_of(r * half, 16), half)
            for f in range(3):
                for p in range(2):
                    at = (p * 3 + f) * stream_local
                    modes[here, at : at + stream_local] = fields[f][p].astype(BF)
            return carry

        lax.fori_loop(0, rows, body, 0)

    by_cosine = dot(cosine[...], modes[...])
    by_sine = dot(sine[...], modes[...])
    part = 3 * stream_local
    pairs = [
        (by_cosine[:, :part], -by_sine[:, part:]),
        (by_cosine[:, part:], by_sine[:, :part]),
    ]
    block = out.shape[3] // 2
    for p, (even, odd) in enumerate(pairs):
        plus = (even + odd).astype(BF)
        minus = (even - odd).astype(BF)
        for d in range(out.shape[0]):
            for f in range(3):
                lanes = slice(f * stream_local, (f + 1) * stream_local)
                out[d, f, p, :block] = plus[d * block : (d + 1) * block, lanes]
                out[d, f, p, block:] = minus[d * block : (d + 1) * block, lanes]


def inverse_span(group, x, stream_wave, split, cosine, sine, col_count):
    rows, sent, stream_local, width = x.shape
    half_points, span_modes = cosine.shape
    block = half_points // col_count
    step = 2
    whole = lambda a: pl.BlockSpec(a.shape, lambda i: (0,) * a.ndim)
    table = pl.BlockSpec((step * block, span_modes), lambda i: (i, 0))
    return pl.pallas_call(
        functools.partial(inverse_kernel, group, span_modes),
        grid=(col_count // step,),
        in_specs=[whole(x), whole(stream_wave), whole(split), table, table],
        out_specs=pl.BlockSpec(
            (step, 3, 2, 2 * block, stream_local), lambda i: (i, 0, 0, 0, 0)
        ),
        out_shape=jax.ShapeDtypeStruct((col_count, 3, 2, 2 * block, stream_local), BF),
        scratch_shapes=[pltpu.VMEM((span_modes, 6 * stream_local), BF)],
        compiler_params=pltpu.CompilerParams(vmem_limit_bytes=VMEM_LIMIT),
        cost_estimate=pl.CostEstimate(
            flops=2 * 12 * stream_local * span_modes * half_points,
            bytes_accessed=4 * half_points * span_modes + 4 * x.size,
            transcendentals=0,
        ),
        name="inverse_span",
    )(x, stream_wave, split, cosine, sine)


def product_kernel(chunk, ga, gb, wave_c, wave_s, back_c, back_s, o0, o1, o2, reals, imags, acc_re, acc_im):
    cols, _, _, _, hb, lanes = ga.shape
    per = 2 * hb
    for g, ref in enumerate((ga, gb)):
        for f in range(3):
            row = (g * 3 + f) * per
            for d in range(cols):
                at = slice(d * lanes, (d + 1) * lanes)
                for s in range(2):
                    reals[row + s * hb : row + (s + 1) * hb, at] = ref[d, f, 0, s]
                    imags[row + s * hb : row + (s + 1) * hb, at] = ref[d, f, 1, s]
    points = wave_c.shape[1]
    for b in range(points // chunk):
        xs = slice(b * chunk, (b + 1) * chunk)
        even = dot(reals[...], wave_c[:, xs])
        odd = dot(imags[...], wave_s[:, xs])
        products = []
        for phys in (even + odd, even - odd):
            u, w, wy, v, wx, wz = [phys[k * per : (k + 1) * per] for k in range(6)]
            products.append((v * wz - w * wy, w * wx - u * wz, u * wy - v * wx))
        sums = []
        diffs = []
        for c in range(3):
            total = products[0][c] + products[1][c]
            gap = products[0][c] - products[1][c]
            sums += [total[:hb] + total[hb:], total[:hb] - total[hb:]]
            diffs += [gap[:hb] + gap[hb:], gap[:hb] - gap[hb:]]
        re = dot(jnp.concatenate(sums, axis=0).astype(BF), back_c[xs, :])
        im = dot(jnp.concatenate(diffs, axis=0).astype(BF), back_s[xs, :])
        if b == 0:
            acc_re[...] = re
            acc_im[...] = im
        else:
            acc_re[...] += re
            acc_im[...] += im
    for c, out in enumerate((o0, o1, o2)):
        for s in range(2):
            row = (c * 2 + s) * hb
            for d in range(cols):
                at = slice(d * lanes, (d + 1) * lanes)
                out[d, 0, s] = acc_re[row : row + hb, at].astype(BF)
                out[d, 1, s] = acc_im[row : row + hb, at].astype(BF)


def products(ga, gb, tables, hb, chunk):
    cols, _, _, points, lanes = ga.shape
    half = points // 2
    shape = (cols, 3, 2, 2, half, lanes)
    ga, gb = ga.reshape(shape), gb.reshape(shape)
    modes = cols * lanes
    spec = pl.BlockSpec((cols, 3, 2, 2, hb, lanes), lambda i: (0, 0, 0, 0, i, 0))
    out_spec = pl.BlockSpec((cols, 2, 2, hb, lanes), lambda i: (0, 0, 0, i, 0))
    whole = lambda a: pl.BlockSpec(a.shape, lambda i: (0, 0), pipeline_mode=pl.Buffered(1))
    stream_half = tables[0].shape[1]
    return pl.pallas_call(
        functools.partial(product_kernel, chunk),
        grid=(half // hb,),
        in_specs=[spec, spec] + [whole(t) for t in tables],
        out_specs=[out_spec] * 3,
        out_shape=[jax.ShapeDtypeStruct((cols, 2, 2, half, lanes), BF)] * 3,
        scratch_shapes=[
            pltpu.VMEM((12 * hb, modes), BF),
            pltpu.VMEM((12 * hb, modes), BF),
            pltpu.VMEM((6 * hb, modes), F32),
            pltpu.VMEM((6 * hb, modes), F32),
        ],
        compiler_params=pltpu.CompilerParams(vmem_limit_bytes=VMEM_LIMIT),
        cost_estimate=pl.CostEstimate(
            flops=2 * 36 * half * modes * stream_half,
            bytes_accessed=8 * modes * stream_half + 36 * 2 * points * modes,
            transcendentals=0,
        ),
        name="products",
    )(ga, gb, *tables)


def finish_kernel(norm, t0, t1, t2, split, cosine, sine, out, got, plus, minus, made, col_send, col_recv, row_send, row_recv, own):
    _, cols, _, _, block, lanes = got.shape
    _, rows, _, width = made.shape
    half = width // 2
    col, row = lax.axis_index("col"), lax.axis_index("row")
    mesh_ids = pl.DeviceIdType.MESH
    col_peers = [lax.rem(col + k, cols) for k in range(1, cols)]
    row_peers = [lax.rem(row + k, rows) for k in range(1, rows)]

    barrier = pltpu.get_barrier_semaphore()
    for peer in col_peers:
        pl.semaphore_signal(barrier, inc=1, device_id={"col": peer}, device_id_type=mesh_ids)
    for peer in row_peers:
        pl.semaphore_signal(barrier, inc=1, device_id={"row": peer}, device_id_type=mesh_ids)
    pl.semaphore_wait(barrier, cols + rows - 2)

    terms = (t0, t1, t2)

    def start_cols(c):
        copies = [pltpu.make_async_copy(terms[c].at[col], got.at[c, col], own.at[0, c])]
        for k, peer in enumerate(col_peers):
            copies.append(
                pltpu.make_async_remote_copy(
                    src_ref=terms[c].at[peer],
                    dst_ref=got.at[c, col],
                    send_sem=col_send.at[c, k],
                    recv_sem=col_recv.at[c, k],
                    device_id={"col": peer},
                    device_id_type=mesh_ids,
                )
            )
        for copy in copies:
            copy.start()
        return copies

    def start_rows(c):
        copies = []
        for k, peer in enumerate(row_peers):
            copies.append(
                pltpu.make_async_remote_copy(
                    src_ref=made.at[c, peer],
                    dst_ref=out.at[c, row],
                    send_sem=row_send.at[c, k],
                    recv_sem=row_recv.at[c, k],
                    device_id={"row": peer},
                    device_id_type=mesh_ids,
                )
            )
        copies.append(pltpu.make_async_copy(made.at[c, row], out.at[c, row], own.at[1, c]))
        for copy in copies:
            copy.start()
        return copies

    sent = []
    moving = start_cols(0)
    for c in range(3):
        for copy in moving:
            copy.wait()
        if c < 2:
            moving = start_cols(c + 1)
        for d in range(cols):
            here = slice(d * block, (d + 1) * block)
            for p in range(2):
                at = slice(p * lanes, (p + 1) * lanes)
                plus[here, at] = got[c, d, p, 0]
                minus[here, at] = got[c, d, p, 1]

        def body(r, carry, c=c):
            at = pl.ds(pl.multiple_of(r * half, 16), half)
            by_cosine = dot(cosine[at, :], plus[...])
            by_sine = dot(sine[at, :], minus[...])
            re = (by_cosine[:, :lanes] + by_sine[:, lanes:]) * norm
            im = (by_cosine[:, lanes:] - by_sine[:, :lanes]) * norm
            parts = jnp.concatenate([re, im], axis=0).astype(BF)
            made[c, r] = lax.dot_general(
                parts, split[...], (((0,), (0,)), ((), ())), preferred_element_type=F32
            ).astype(BF)
            return carry

        lax.fori_loop(0, rows, body, 0)
        sent += start_rows(c)
    for copy in sent:
        copy.wait()


def finish(terms, split, cosine, sine, norm, row_count):
    cols, _, _, block, lanes = terms[0].shape
    span_modes, half_points = cosine.shape
    width = 2 * span_modes // row_count
    hbm = pl.BlockSpec(memory_space=pl.ANY)
    vmem = pl.BlockSpec(memory_space=pltpu.VMEM)
    return pl.pallas_call(
        functools.partial(finish_kernel, norm),
        in_specs=[hbm] * 3 + [vmem] * 3,
        out_specs=hbm,
        out_shape=jax.ShapeDtypeStruct((3, row_count, lanes, width), BF),
        scratch_shapes=[
            pltpu.VMEM((3,) + terms[0].shape, BF),
            pltpu.VMEM((half_points, 2 * lanes), BF),
            pltpu.VMEM((half_points, 2 * lanes), BF),
            pltpu.VMEM((3, row_count, lanes, width), BF),
            pltpu.SemaphoreType.DMA((3, cols - 1)),
            pltpu.SemaphoreType.DMA((3, cols - 1)),
            pltpu.SemaphoreType.DMA((3, row_count - 1)),
            pltpu.SemaphoreType.DMA((3, row_count - 1)),
            pltpu.SemaphoreType.DMA((2, 3)),
        ],
        compiler_params=pltpu.CompilerParams(
            collective_id=0, has_side_effects=True, vmem_limit_bytes=VMEM_LIMIT
        ),
        cost_estimate=pl.CostEstimate(
            flops=2 * 12 * lanes * span_modes * half_points,
            bytes_accessed=4 * half_points * span_modes + 24 * terms[0].size,
            transcendentals=0,
        ),
        name="finish",
    )(*terms, split, cosine, sine)


def exchange(x, axis):
    return lax.all_to_all(x, axis, split_axis=0, concat_axis=0, tiled=True)


def on_device(coefficients, basis_values, basis_slopes, band_offsets):
    row_count = lax.axis_size("row")
    col_count = lax.axis_size("col")
    stream_local = coefficients.shape[2]
    span_local = coefficients.shape[3] // 2
    stream_modes = stream_local * col_count
    span_modes = span_local * row_count
    span_points = 3 * span_modes // 2
    stream_points = 3 * stream_modes
    cosine, sine = span_tables(span_modes, span_points)
    wave_c, wave_s = stream_tables(stream_modes, stream_points)
    weight = np.where(np.arange(stream_modes) == 0, 1.0, 2.0)[:, None].astype(ml_dtypes.bfloat16)
    stream = [wave_c * weight, wave_s * weight, wave_c.T, wave_s.T]
    stream = [jnp.asarray(np.ascontiguousarray(t)) for t in stream]
    split = jnp.asarray(split_table(span_local))
    span = jnp.asarray(cosine), jnp.asarray(sine)
    back = jnp.asarray(np.ascontiguousarray(cosine.T)), jnp.asarray(np.ascontiguousarray(sine.T))
    norm = 1.0 / (stream_points * span_points)

    stream_index = lax.axis_index("col") * stream_local + jnp.arange(stream_local, dtype=jnp.int32)
    stream_wave = (stream_index.astype(F32) * stream_unit)[None, :]

    sent = collocate(coefficients, basis_values, basis_slopes, band_offsets, 32)
    grids = []
    for group in range(2):
        modes = exchange(sent[group], "row")
        grid = inverse_span(group, modes, stream_wave, split, *span, col_count)
        grids.append(exchange(grid, "col"))
    half = span_points // 2 // col_count
    terms = products(*grids, stream, 48 if half % 48 == 0 else half, 512)
    return finish(terms, split, *back, norm, row_count).astype(F32)


def solution(mesh):
    placed = (P(None, None, "col", "row"), P(), P(), P())
    return jax.shard_map(
        on_device,
        mesh=mesh,
        in_specs=placed,
        out_specs=P(None, None, "col", "row"),
        check_vma=False,
    )
```

```python
import functools
import math

import jax
import jax.numpy as jnp
import ml_dtypes
import numpy as np
from jax import lax
from jax.experimental import pallas as pl
from jax.experimental.pallas import tpu as pltpu
from jax.sharding import PartitionSpec as P

stream_unit = 0.25
span_unit = 2.0 / 3.0
VMEM_LIMIT = 56 * 1024 * 1024
BF = jnp.bfloat16
F32 = jnp.float32


def span_tables(mode_total, points):
    mode = np.arange(mode_total)
    signed = np.where(mode < mode_total // 2, mode, mode - mode_total)
    odd = 2 * np.arange(points // 2) + 1
    angle = np.mod(odd[:, None] * signed[None, :], 2 * points) * (math.pi / points)
    return np.cos(angle).astype(ml_dtypes.bfloat16), np.sin(angle).astype(ml_dtypes.bfloat16)


def stream_tables(mode_total, points):
    mode = np.arange(mode_total)
    odd = 2 * np.arange(points // 2) + 1
    angle = np.mod(mode[:, None] * odd[None, :], 2 * points) * (math.pi / points)
    return np.cos(angle).astype(ml_dtypes.bfloat16), (-np.sin(angle)).astype(ml_dtypes.bfloat16)


def split_table(count):
    table = np.zeros((2, count, 2 * count), ml_dtypes.bfloat16)
    index = np.arange(count)
    table[0, index, 2 * index] = 1
    table[1, index, 2 * index + 1] = 1
    return table.reshape(2 * count, 2 * count)


def dot(left, right):
    return jnp.dot(left, right, preferred_element_type=F32)


def collocate_kernel(values, slopes, offsets, coef, first, second):
    planes = values.shape[0]
    for j in range(planes):
        base = offsets[j]

        def total(weights, c):
            return sum(
                weights[j, t] * coef[c, base + t] for t in range(weights.shape[1])
            ).astype(BF)

        first[j, 0] = total(values, 0)
        first[j, 1] = total(values, 2)
        second[j, 0] = total(values, 1)
        second[j, 1] = total(slopes, 0)
        second[j, 2] = total(slopes, 2)


def collocate(coefficients, values, slopes, offsets, rows):
    _, splines, stream_local, width = coefficients.shape
    planes = values.shape[0]
    smem = pl.BlockSpec(memory_space=pltpu.SMEM)
    return pl.pallas_call(
        collocate_kernel,
        grid=(stream_local // rows,),
        in_specs=[smem, smem, smem, pl.BlockSpec((3, splines, rows, width), lambda i: (0, 0, i, 0))],
        out_specs=[
            pl.BlockSpec((planes, 2, rows, width), lambda i: (0, 0, i, 0)),
            pl.BlockSpec((planes, 3, rows, width), lambda i: (0, 0, i, 0)),
        ],
        out_shape=[
            jax.ShapeDtypeStruct((planes, 2, stream_local, width), BF),
            jax.ShapeDtypeStruct((planes, 3, stream_local, width), BF),
        ],
        compiler_params=pltpu.CompilerParams(vmem_limit_bytes=VMEM_LIMIT),
        name="collocate",
    )(values, slopes, offsets, coefficients)


def lift_modes(group, span_modes, x, stream_wave, split, modes):
    rows, sent, stream_local, width = x.shape
    half = width // 2
    wave_x = stream_wave[...]

    def body(r, carry):
        flat = x[r].reshape(sent * stream_local, width)
        parts = lax.dot_general(
            split[...], flat, (((1,), (1,)), ((), ())), preferred_element_type=F32
        )
        field = lambda k: (
            parts[:half, k * stream_local : (k + 1) * stream_local],
            parts[half:, k * stream_local : (k + 1) * stream_local],
        )
        mode = r * half + lax.broadcasted_iota(jnp.int32, (half, stream_local), 0)
        signed = jnp.where(mode < span_modes // 2, mode, mode - span_modes)
        wave_z = signed.astype(F32) * span_unit
        if group == 0:
            (ur, ui), (wr, wi) = field(0), field(1)
            fields = [
                (ur, ui),
                (wr, wi),
                (-(wave_x * wi - wave_z * ui), wave_x * wr - wave_z * ur),
            ]
        else:
            (vr, vi), (sur, sui), (swr, swi) = field(0), field(1), field(2)
            fields = [
                (vr, vi),
                (-wave_z * vi - swr, wave_z * vr - swi),
                (sur + wave_x * vi, sui - wave_x * vr),
            ]
        here = pl.ds(pl.multiple_of(r * half, 16), half)
        for f in range(3):
            for p in range(2):
                at = (p * 3 + f) * stream_local
                modes[here, at : at + stream_local] = fields[f][p].astype(BF)
        return carry

    lax.fori_loop(0, rows, body, 0)


def start_kernel(
    a, b, stream_wave, split, cosine, sine, ga, gb,
    xa, xb, modes, made, row_send, row_recv, col_send, col_recv, own,
):
    rows, _, stream_local, _ = xa.shape
    cols = ga.shape[0]
    pairs = cols // 2
    block = ga.shape[3] // 2
    span_modes = cosine.shape[1]
    col, row = lax.axis_index("col"), lax.axis_index("row")
    pair, core = col // 2, lax.rem(col, 2)
    mesh_ids = pl.DeviceIdType.MESH
    row_peers = [lax.rem(row + k, rows) for k in range(1, rows)]

    barrier = pltpu.get_barrier_semaphore()
    for k in range(1, cols):
        peer = lax.rem(col + k, cols)
        pl.semaphore_signal(barrier, inc=1, device_id={"col": peer}, device_id_type=mesh_ids)
    for peer in row_peers:
        pl.semaphore_signal(barrier, inc=1, device_id={"row": peer}, device_id_type=mesh_ids)
    pl.semaphore_wait(barrier, cols + rows - 2)

    def start_rows(g):
        source, target = ((a, xa), (b, xb))[g]
        copies = [pltpu.make_async_copy(source.at[row], target.at[row], own.at[0, g])]
        for k, peer in enumerate(row_peers):
            copies.append(
                pltpu.make_async_remote_copy(
                    src_ref=source.at[peer],
                    dst_ref=target.at[row],
                    send_sem=row_send.at[g, k],
                    recv_sem=row_recv.at[g, k],
                    device_id={"row": peer},
                    device_id_type=mesh_ids,
                )
            )
        for copy in copies:
            copy.start()
        return copies

    def start_col(g, turn, other):
        to_pair = lax.rem(pair + turn, pairs)
        peer = to_pair * 2 + lax.rem(core + other, 2)
        grid = (ga, gb)[g]
        if turn == 0 and other == 0:
            copy = pltpu.make_async_copy(made.at[g, col], grid.at[col], own.at[1, g])
        else:
            copy = pltpu.make_async_remote_copy(
                src_ref=made.at[g, peer],
                dst_ref=grid.at[col],
                send_sem=col_send.at[g, turn, other],
                recv_sem=col_recv.at[g, turn, other],
                device_id={"col": peer},
                device_id_type=mesh_ids,
            )
        copy.start()
        return copy

    part = 3 * stream_local
    sent = []
    moving = start_rows(0)
    for g in range(2):
        for copy in moving:
            copy.wait()
        if g == 0:
            moving = start_rows(1)
        lift_modes(g, span_modes, (xa, xb)[g], stream_wave, split, modes)
        for step in range(pairs):
            turn = (step + 1) % pairs
            to_pair = lax.rem(pair + turn, pairs)
            at = pl.ds(pl.multiple_of(to_pair * 2 * block, 16), 2 * block)
            by_cosine = dot(cosine[at, :], modes[...])
            by_sine = dot(sine[at, :], modes[...])
            sums = [
                (by_cosine[:, :part], -by_sine[:, part:]),
                (by_cosine[:, part:], by_sine[:, :part]),
            ]
            for p, (even, odd) in enumerate(sums):
                plus = (even + odd).astype(BF)
                minus = (even - odd).astype(BF)
                for d in range(2):
                    for f in range(3):
                        lanes = slice(f * stream_local, (f + 1) * stream_local)
                        made[g, to_pair * 2 + d, f, p, :block] = plus[d * block : (d + 1) * block, lanes]
                        made[g, to_pair * 2 + d, f, p, block:] = minus[d * block : (d + 1) * block, lanes]
            for other in range(2):
                sent.append(start_col(g, turn, other))
    for copy in sent:
        copy.wait()


def start(sent, stream_wave, split, cosine, sine, col_count):
    a, b = sent
    rows, _, stream_local, _ = a.shape
    half_points, span_modes = cosine.shape
    block = half_points // col_count
    hbm = pl.BlockSpec(memory_space=pl.ANY)
    vmem = pl.BlockSpec(memory_space=pltpu.VMEM)
    grid = (col_count, 3, 2, 2 * block, stream_local)
    return pl.pallas_call(
        start_kernel,
        in_specs=[hbm] * 2 + [vmem] * 4,
        out_specs=[hbm] * 2,
        out_shape=[jax.ShapeDtypeStruct(grid, BF)] * 2,
        scratch_shapes=[
            pltpu.VMEM(a.shape, BF),
            pltpu.VMEM(b.shape, BF),
            pltpu.VMEM((span_modes, 6 * stream_local), BF),
            pltpu.VMEM((2,) + grid, BF),
            pltpu.SemaphoreType.DMA((2, rows - 1)),
            pltpu.SemaphoreType.DMA((2, rows - 1)),
            pltpu.SemaphoreType.DMA((2, col_count // 2, 2)),
            pltpu.SemaphoreType.DMA((2, col_count // 2, 2)),
            pltpu.SemaphoreType.DMA((2, 2)),
        ],
        compiler_params=pltpu.CompilerParams(
            collective_id=1, has_side_effects=True, vmem_limit_bytes=VMEM_LIMIT
        ),
        cost_estimate=pl.CostEstimate(
            flops=2 * 24 * stream_local * span_modes * half_points,
            bytes_accessed=4 * half_points * span_modes + 4 * (a.size + b.size),
            transcendentals=0,
        ),
        name="start",
    )(a, b, stream_wave, split, cosine, sine)


def product_kernel(chunk, ga, gb, wave_c, wave_s, back_c, back_s, o0, o1, o2, reals, imags, acc_re, acc_im):
    cols, _, _, _, hb, lanes = ga.shape
    per = 2 * hb
    for g, ref in enumerate((ga, gb)):
        for f in range(3):
            row = (g * 3 + f) * per
            for d in range(cols):
                at = slice(d * lanes, (d + 1) * lanes)
                for s in range(2):
                    reals[row + s * hb : row + (s + 1) * hb, at] = ref[d, f, 0, s]
                    imags[row + s * hb : row + (s + 1) * hb, at] = ref[d, f, 1, s]
    points = wave_c.shape[1]
    for b in range(points // chunk):
        xs = slice(b * chunk, (b + 1) * chunk)
        even = dot(reals[...], wave_c[:, xs])
        odd = dot(imags[...], wave_s[:, xs])
        products = []
        for phys in (even + odd, even - odd):
            u, w, wy, v, wx, wz = [phys[k * per : (k + 1) * per] for k in range(6)]
            products.append((v * wz - w * wy, w * wx - u * wz, u * wy - v * wx))
        sums = []
        diffs = []
        for c in range(3):
            total = products[0][c] + products[1][c]
            gap = products[0][c] - products[1][c]
            sums += [total[:hb] + total[hb:], total[:hb] - total[hb:]]
            diffs += [gap[:hb] + gap[hb:], gap[:hb] - gap[hb:]]
        re = dot(jnp.concatenate(sums, axis=0).astype(BF), back_c[xs, :])
        im = dot(jnp.concatenate(diffs, axis=0).astype(BF), back_s[xs, :])
        if b == 0:
            acc_re[...] = re
            acc_im[...] = im
        else:
            acc_re[...] += re
            acc_im[...] += im
    for c, out in enumerate((o0, o1, o2)):
        for s in range(2):
            row = (c * 2 + s) * hb
            for d in range(cols):
                at = slice(d * lanes, (d + 1) * lanes)
                out[d, 0, s] = acc_re[row : row + hb, at].astype(BF)
                out[d, 1, s] = acc_im[row : row + hb, at].astype(BF)


def products(ga, gb, tables, hb, chunk):
    cols, _, _, points, lanes = ga.shape
    half = points // 2
    shape = (cols, 3, 2, 2, half, lanes)
    ga, gb = ga.reshape(shape), gb.reshape(shape)
    modes = cols * lanes
    spec = pl.BlockSpec((cols, 3, 2, 2, hb, lanes), lambda i: (0, 0, 0, 0, i, 0))
    out_spec = pl.BlockSpec((cols, 2, 2, hb, lanes), lambda i: (0, 0, 0, i, 0))
    whole = lambda a: pl.BlockSpec(a.shape, lambda i: (0, 0), pipeline_mode=pl.Buffered(1))
    stream_half = tables[0].shape[1]
    return pl.pallas_call(
        functools.partial(product_kernel, chunk),
        grid=(half // hb,),
        in_specs=[spec, spec] + [whole(t) for t in tables],
        out_specs=[out_spec] * 3,
        out_shape=[jax.ShapeDtypeStruct((cols, 2, 2, half, lanes), BF)] * 3,
        scratch_shapes=[
            pltpu.VMEM((12 * hb, modes), BF),
            pltpu.VMEM((12 * hb, modes), BF),
            pltpu.VMEM((6 * hb, modes), F32),
            pltpu.VMEM((6 * hb, modes), F32),
        ],
        compiler_params=pltpu.CompilerParams(vmem_limit_bytes=VMEM_LIMIT),
        cost_estimate=pl.CostEstimate(
            flops=2 * 36 * half * modes * stream_half,
            bytes_accessed=8 * modes * stream_half + 36 * 2 * points * modes,
            transcendentals=0,
        ),
        name="products",
    )(ga, gb, *tables)


def finish_kernel(norm, t0, t1, t2, split, cosine, sine, out, got, plus, minus, made, col_send, col_recv, row_send, row_recv, own):
    _, cols, _, _, block, lanes = got.shape
    _, rows, _, width = made.shape
    half = width // 2
    col, row = lax.axis_index("col"), lax.axis_index("row")
    mesh_ids = pl.DeviceIdType.MESH
    col_peers = [lax.rem(col + k, cols) for k in range(1, cols)]
    row_peers = [lax.rem(row + k, rows) for k in range(1, rows)]

    barrier = pltpu.get_barrier_semaphore()
    for peer in col_peers:
        pl.semaphore_signal(barrier, inc=1, device_id={"col": peer}, device_id_type=mesh_ids)
    for peer in row_peers:
        pl.semaphore_signal(barrier, inc=1, device_id={"row": peer}, device_id_type=mesh_ids)
    pl.semaphore_wait(barrier, cols + rows - 2)

    terms = (t0, t1, t2)

    def start_cols(c):
        copies = [pltpu.make_async_copy(terms[c].at[col], got.at[c, col], own.at[0, c])]
        for k, peer in enumerate(col_peers):
            copies.append(
                pltpu.make_async_remote_copy(
                    src_ref=terms[c].at[peer],
                    dst_ref=got.at[c, col],
                    send_sem=col_send.at[c, k],
                    recv_sem=col_recv.at[c, k],
                    device_id={"col": peer},
                    device_id_type=mesh_ids,
                )
            )
        for copy in copies:
            copy.start()
        return copies

    def start_rows(c):
        copies = []
        for k, peer in enumerate(row_peers):
            copies.append(
                pltpu.make_async_remote_copy(
                    src_ref=made.at[c, peer],
                    dst_ref=out.at[c, row],
                    send_sem=row_send.at[c, k],
                    recv_sem=row_recv.at[c, k],
                    device_id={"row": peer},
                    device_id_type=mesh_ids,
                )
            )
        copies.append(pltpu.make_async_copy(made.at[c, row], out.at[c, row], own.at[1, c]))
        for copy in copies:
            copy.start()
        return copies

    sent = []
    moving = start_cols(0)
    for c in range(3):
        for copy in moving:
            copy.wait()
        if c < 2:
            moving = start_cols(c + 1)
        for d in range(cols):
            here = slice(d * block, (d + 1) * block)
            for p in range(2):
                at = slice(p * lanes, (p + 1) * lanes)
                plus[here, at] = got[c, d, p, 0]
                minus[here, at] = got[c, d, p, 1]

        def body(r, carry, c=c):
            at = pl.ds(pl.multiple_of(r * half, 16), half)
            by_cosine = dot(cosine[at, :], plus[...])
            by_sine = dot(sine[at, :], minus[...])
            re = (by_cosine[:, :lanes] + by_sine[:, lanes:]) * norm
            im = (by_cosine[:, lanes:] - by_sine[:, :lanes]) * norm
            parts = jnp.concatenate([re, im], axis=0).astype(BF)
            made[c, r] = lax.dot_general(
                parts, split[...], (((0,), (0,)), ((), ())), preferred_element_type=F32
            ).astype(BF)
            return carry

        lax.fori_loop(0, rows, body, 0)
        sent += start_rows(c)
    for copy in sent:
        copy.wait()


def finish(terms, split, cosine, sine, norm, row_count):
    cols, _, _, block, lanes = terms[0].shape
    span_modes, half_points = cosine.shape
    width = 2 * span_modes // row_count
    hbm = pl.BlockSpec(memory_space=pl.ANY)
    vmem = pl.BlockSpec(memory_space=pltpu.VMEM)
    return pl.pallas_call(
        functools.partial(finish_kernel, norm),
        in_specs=[hbm] * 3 + [vmem] * 3,
        out_specs=hbm,
        out_shape=jax.ShapeDtypeStruct((3, row_count, lanes, width), BF),
        scratch_shapes=[
            pltpu.VMEM((3,) + terms[0].shape, BF),
            pltpu.VMEM((half_points, 2 * lanes), BF),
            pltpu.VMEM((half_points, 2 * lanes), BF),
            pltpu.VMEM((3, row_count, lanes, width), BF),
            pltpu.SemaphoreType.DMA((3, cols - 1)),
            pltpu.SemaphoreType.DMA((3, cols - 1)),
            pltpu.SemaphoreType.DMA((3, row_count - 1)),
            pltpu.SemaphoreType.DMA((3, row_count - 1)),
            pltpu.SemaphoreType.DMA((2, 3)),
        ],
        compiler_params=pltpu.CompilerParams(
            collective_id=0, has_side_effects=True, vmem_limit_bytes=VMEM_LIMIT
        ),
        cost_estimate=pl.CostEstimate(
            flops=2 * 12 * lanes * span_modes * half_points,
            bytes_accessed=4 * half_points * span_modes + 24 * terms[0].size,
            transcendentals=0,
        ),
        name="finish",
    )(*terms, split, cosine, sine)


def on_device(coefficients, basis_values, basis_slopes, band_offsets):
    row_count = lax.axis_size("row")
    col_count = lax.axis_size("col")
    stream_local = coefficients.shape[2]
    span_local = coefficients.shape[3] // 2
    stream_modes = stream_local * col_count
    span_modes = span_local * row_count
    span_points = 3 * span_modes // 2
    stream_points = 3 * stream_modes
    cosine, sine = span_tables(span_modes, span_points)
    wave_c, wave_s = stream_tables(stream_modes, stream_points)
    weight = np.where(np.arange(stream_modes) == 0, 1.0, 2.0)[:, None].astype(ml_dtypes.bfloat16)
    stream = [wave_c * weight, wave_s * weight, wave_c.T, wave_s.T]
    stream = [jnp.asarray(np.ascontiguousarray(t)) for t in stream]
    split = jnp.asarray(split_table(span_local))
    span = jnp.asarray(cosine), jnp.asarray(sine)
    back = jnp.asarray(np.ascontiguousarray(cosine.T)), jnp.asarray(np.ascontiguousarray(sine.T))
    norm = 1.0 / (stream_points * span_points)

    stream_index = lax.axis_index("col") * stream_local + jnp.arange(stream_local, dtype=jnp.int32)
    stream_wave = (stream_index.astype(F32) * stream_unit)[None, :]

    sent = collocate(coefficients, basis_values, basis_slopes, band_offsets, 32)
    grids = start(sent, stream_wave, split, *span, col_count)
    half = span_points // 2 // col_count
    terms = products(*grids, stream, 48 if half % 48 == 0 else half, 512)
    return finish(terms, split, *back, norm, row_count).astype(F32)


def solution(mesh):
    placed = (P(None, None, "col", "row"), P(), P(), P())
    return jax.shard_map(
        on_device,
        mesh=mesh,
        in_specs=placed,
        out_specs=P(None, None, "col", "row"),
        check_vma=False,
    )
```
